32 devices in a mesh: lon: 4 (over z), lev: 2 (over x), lat: 4 (over y, core).
Axes of the slice: x: 2, y: 2, z: 4, core: 2. Of those that a mesh axis runs over, the one named last changes fastest.
Arguments:
- features: bfloat16 [32, 128, 8, 192], P('lat', 'lon', 'lev'), may hold values from -6 to 6
- conv_weight: bfloat16 [8, 3, 3, 192, 192], P('lev'), may hold values from -0.15625 to 0.15625
- join_weight: bfloat16 [8, 192, 8, 192], replicated, may hold values from -0.15625 to 0.15625
- joined_grad: bfloat16 [32, 128, 8, 192], P('lat', 'lon', 'lev'), may hold values from -6 to 6
Outputs:
- joined_fields: float32 [32, 128, 8, 192], P('lat', 'lon', 'lev')
- input_grad: float32 [32, 128, 8, 192], P('lat', 'lon', 'lev')
- conv_grad: float32 [8, 3, 3, 192, 192], P('lev', None, None, 'lon')
- join_grad: float32 [8, 192, 8, 192], P(None, 'lon', 'lev')
The draws below stay inside these ranges and needn't reach their ends.
All inputs are finite; a program needn't handle non-finite values.
Results may differ from the reference program's by a relative error of at most 0.0029.
Values may be sent and summed in bfloat16 or wider, within the bound.
A program may use at most 128 MiB of HBM per device.

```python
import math
from functools import partial
import jax
import jax.numpy as jnp
from jax import lax

C = 192
LEV = 8
NLAT = 32
NLON = 128


def steps_of(key, extent, pieces, low, top_value):
    gain = 1.0
    for position, blocks in pieces:
        heights = jax.random.uniform(jax.random.fold_in(jax.random.fold_in(key, 6), position), (blocks,), jnp.float32, low / len(pieces), top_value / len(pieces))
        gain = gain * jnp.repeat(jnp.exp(heights), extent[position] // blocks).reshape((-1,) + (1,) * (len(extent) - 1 - position))
    return gain


def scatter_about(own_key, shape, scale, bound, split=(), held_as=jnp.bfloat16):
    drawn = jax.random.normal(own_key, shape, jnp.float32) * scale
    if len(split) > 0:
        drawn = steps_of(own_key, shape, split, -0.22, 0.18) * drawn
    return jnp.clip(drawn, min=-bound, max=bound).astype(held_as)


def setup_inputs(seed: int = 0) -> dict:
    key_list = jax.random.split(jax.random.key(seed), 5)
    return {
        "features": scatter_about(key_list[0], (NLAT, NLON, LEV, C), 1.0, 6.0, ((0, 4), (1, 4), (2, 2))),
        "conv_weight": scatter_about(key_list[1], (LEV, 3, 3, C, C), (9 * C) ** -0.5, 0.15625, ((0, 2),)),
        "join_weight": scatter_about(key_list[2], (LEV, C, LEV, C), (LEV * C) ** -0.5, 0.15625),
        "joined_grad": scatter_about(key_list[3], (NLAT, NLON, LEV, C), 1.0, 6.0, ((0, 4), (1, 4), (2, 2))),
    }


def extend_level(plane):
    lon_wide = jnp.concatenate([plane[:, -1:], plane, plane[:, :1]], axis=1)
    return jnp.pad(lon_wide, ((1, 1), (0, 0), (0, 0)))

def level_forward(operands):
    plane, weight = operands
    padded = extend_level(plane).astype(jnp.float32)
    kernel = weight.astype(jnp.float32)
    summed = jnp.zeros((plane.shape[0], plane.shape[1], kernel.shape[3]), jnp.float32)
    for tap_row in range(3):
        for tap_col in range(3):
            window = padded[tap_row:tap_row + plane.shape[0], tap_col:tap_col + plane.shape[1]]
            summed = summed + jnp.einsum('abi,io->abo', window, kernel[tap_row, tap_col])
    return summed

def level_backward(operands):
    plane_grad, weight = operands
    padded = extend_level(plane_grad).astype(jnp.float32)
    kernel = weight.astype(jnp.float32)
    summed = jnp.zeros((plane_grad.shape[0], plane_grad.shape[1], kernel.shape[2]), jnp.float32)
    for tap_row in range(3):
        for tap_col in range(3):
            window = padded[2 - tap_row:2 - tap_row + plane_grad.shape[0], 2 - tap_col:2 - tap_col + plane_grad.shape[1]]
            summed = summed + jnp.einsum('abo,io->abi', window, kernel[tap_row, tap_col])
    return summed

def level_weight(operands):
    plane, plane_grad = operands
    padded = extend_level(plane).astype(jnp.float32)
    grad_value = plane_grad.astype(jnp.float32)
    rows_list = []
    for tap_row in range(3):
        tap_list = []
        for tap_col in range(3):
            window = padded[tap_row:tap_row + plane.shape[0], tap_col:tap_col + plane.shape[1]]
            tap_list.append(jnp.einsum('abi,abo->io', window, grad_value))
        rows_list.append(jnp.stack(tap_list, axis=0))
    return jnp.stack(rows_list, axis=0)

def reference(features, conv_weight, join_weight, joined_grad):
    by_level = jnp.moveaxis(features, 2, 0)
    pre_act = jnp.moveaxis(lax.map(level_forward, (by_level, conv_weight)), 0, 2)
    gelu_out, pull_back = jax.vjp(partial(jax.nn.gelu, approximate=True), pre_act)
    activation = gelu_out.astype(jnp.bfloat16)
    flat_act = activation.reshape(NLAT * NLON, LEV * C)
    flat_weight = join_weight.reshape(LEV * C, LEV * C)
    joined_fields = jnp.dot(flat_act, flat_weight, preferred_element_type=jnp.float32).reshape(features.shape)
    flat_grad = joined_grad.reshape(NLAT * NLON, LEV * C)
    act_grad = jnp.dot(flat_grad, flat_weight.T, preferred_element_type=jnp.float32).reshape(features.shape)
    pre_grad = pull_back(act_grad)[0].astype(jnp.bfloat16)
    grad_levels = jnp.moveaxis(pre_grad, 2, 0)
    input_grad = jnp.moveaxis(lax.map(level_backward, (grad_levels, conv_weight)), 0, 2)
    grid_scale = 1.0 / math.sqrt(NLAT * NLON)
    conv_grad = lax.map(level_weight, (by_level, grad_levels)) * grid_scale
    join_grad = jnp.dot(flat_act.T, flat_grad, preferred_element_type=jnp.float32).reshape(LEV, C, LEV, C) * grid_scale
    return (joined_fields, input_grad, conv_grad, join_grad)
```

```python
import math

import jax
import jax.numpy as jnp
from jax import lax
from jax.experimental import pallas as pl
from jax.experimental.pallas import tpu as pltpu
from jax.sharding import PartitionSpec as P

F32 = jnp.float32
BF16 = jnp.bfloat16
MESH = pl.DeviceIdType.MESH
ROOT = math.sqrt(2.0 / math.pi)


def dot(a, b, a_dim, b_dim):
    return lax.dot_general(a, b, (((a_dim,), (b_dim,)), ((), ())), preferred_element_type=F32)


def make_kernel(n_lon, n_lat, rows, cols, levs, chans, scale):
    share = chans // n_lon
    cells = rows * cols
    wide = levs * chans

    def kernel(
        x_ref, cw_ref, jw_ref, jg_ref,
        jf_ref, ig_ref, gj_ref, gc_ref,
        jg_in, edge_out, edge_in, xs, ps, act, act_in, ag,
        own_a, s1_a, r1_a, s2_a, r2_a, s3_a, r3_a, g_a,
        own_b, s1_b, r1_b, s2_b, r2_b, s3_b, r3_b, g_b,
        own_c, s1_c, r1_c, s2_c, r2_c, s3_c, r3_c, g_c,
        lev_send, lev_recv, edge_send, edge_recv, lat_send, lat_recv,
        p1_send, p1_recv, p2_send, p2_recv, p3_send, p3_recv,
        p4_send, p4_recv, p5_send, p5_recv,
    ):
        z = lax.axis_index("lon")
        e = lax.axis_index("lev")
        t = lax.axis_index("lat")
        y = t // 2
        core = lax.rem(t, 2)
        right = lax.rem(z + 1, n_lon)
        left = lax.rem(z + n_lon - 1, n_lon)
        sibling = 2 * y + (1 - core)
        across = 2 * (1 - y) + core

        barrier = pltpu.get_barrier_semaphore()
        for d in range(1, n_lon):
            pl.semaphore_signal(
                barrier, inc=1, device_id={"lon": lax.rem(z + d, n_lon)}, device_id_type=MESH
            )
        for d in range(1, n_lat):
            pl.semaphore_signal(
                barrier, inc=1, device_id={"lat": lax.rem(t + d, n_lat)}, device_id_type=MESH
            )
        pl.semaphore_signal(barrier, inc=1, device_id={"lev": 1 - e}, device_id_type=MESH)
        pl.semaphore_wait(barrier, n_lon + n_lat - 1)

        def remote(src, dst, send, recv, where):
            return pltpu.make_async_remote_copy(
                src_ref=src, dst_ref=dst, send_sem=send, recv_sem=recv,
                device_id=where, device_id_type=MESH,
            )

        jg_copy = remote(jg_ref, jg_in, lev_send.at[0], lev_recv.at[0], {"lev": 1 - e})
        jg_copy.start()

        def edge_copies(n):
            return (
                remote(
                    edge_out.at[2 * n], edge_in.at[2 * n],
                    edge_send.at[2 * n], edge_recv.at[2 * n], {"lon": right},
                ),
                remote(
                    edge_out.at[2 * n + 1], edge_in.at[2 * n + 1],
                    edge_send.at[2 * n + 1], edge_recv.at[2 * n + 1], {"lon": left},
                ),
            )

        def put_middle(n, dst, l, value):
            edge_out[2 * n, l] = value[:, cols - 1, :]
            edge_out[2 * n + 1, l] = value[:, 0, :]
            dst[1 : rows + 1, 1, l] = value.astype(BF16)

        def put_sides(n, dst):
            @pl.loop(0, levs)
            def _(l):
                value = dst[1 : rows + 1, 1, l].astype(F32)
                before = edge_in[2 * n, l].reshape(rows, 1, chans)
                after = edge_in[2 * n + 1, l].reshape(rows, 1, chans)
                dst[1 : rows + 1, 0, l] = jnp.concatenate(
                    [before, value[:, : cols - 1]], axis=1
                ).astype(BF16)
                dst[1 : rows + 1, 2, l] = jnp.concatenate(
                    [value[:, 1:], after], axis=1
                ).astype(BF16)

        def lat_down(n, dst):
            return remote(
                dst.at[rows], dst.at[0], lat_send.at[2 * n], lat_recv.at[2 * n], {"lat": t + 1}
            )

        def lat_up(n, dst):
            return remote(
                dst.at[1], dst.at[rows + 1],
                lat_send.at[2 * n + 1], lat_recv.at[2 * n + 1], {"lat": t - 1},
            )

        def lat_start(n, dst):
            @pl.when(t < n_lat - 1)
            def _():
                lat_down(n, dst).start()

            @pl.when(t > 0)
            def _():
                lat_up(n, dst).start()

            @pl.when(t == 0)
            def _():
                dst[0] = jnp.zeros(dst.shape[1:], BF16)

            @pl.when(t == n_lat - 1)
            def _():
                dst[rows + 1] = jnp.zeros(dst.shape[1:], BF16)

        def lat_wait(n, dst):
            @pl.when(t < n_lat - 1)
            def _():
                lat_down(n, dst).wait_send()
                lat_up(n, dst).wait_recv()

            @pl.when(t > 0)
            def _():
                lat_up(n, dst).wait_send()
                lat_down(n, dst).wait_recv()

        @pl.loop(0, levs)
        def _(l):
            put_middle(0, xs, l, x_ref[l].astype(F32))

        edges = edge_copies(0)
        for c in edges:
            c.start()

        @pl.loop(0, levs)
        def _(l):
            block = jw_ref[e * levs + l, :, pl.ds(pl.multiple_of(e * wide, 128), wide)]
            ag[l] = dot(jg_ref[...], block, 1, 1)

        for c in edges:
            c.wait()
        put_sides(0, xs)
        lat_start(0, xs)

        jg_copy.wait()

        @pl.loop(0, levs)
        def _(l):
            block = jw_ref[e * levs + l, :, pl.ds(pl.multiple_of((1 - e) * wide, 128), wide)]
            ag[l] += dot(jg_in[...], block, 1, 1)

        lat_wait(0, xs)

        @pl.loop(0, levs)
        def _(l):
            total = None
            for p in range(3):
                for q in range(3):
                    window = xs[p : p + rows, q, l].reshape(cells, chans)
                    term = dot(window, cw_ref[l, p, q], 1, 0)
                    total = term if total is None else total + term
            square = total * total
            bent = jnp.tanh(ROOT * (total + 0.044715 * total * square))
            half = 0.5 * (1.0 + bent)
            act[l] = (total * half).astype(BF16)
            slope = half + 0.5 * total * (1.0 - bent * bent) * (
                ROOT * (1.0 + 3.0 * 0.044715 * square)
            )
            grad = (ag[l] * slope).astype(BF16).astype(F32)
            put_middle(1, ps, l, grad.reshape(rows, cols, chans))

        act_copy = remote(act, act_in, lev_send.at[1], lev_recv.at[1], {"lev": 1 - e})
        act_copy.start()
        edges_g = edge_copies(1)
        for c in edges_g:
            c.start()

        class Round:
            def __init__(self, n, bufs):
                self.n = n
                self.own, self.s1, self.r1, self.s2, self.r2, self.s3, self.r3, self.g = bufs
                n3 = n * (n_lon - 1)
                self.c1 = remote(
                    self.s1, self.r1, p1_send.at[n], p1_recv.at[n], {"lat": sibling}
                )
                self.c2 = remote(
                    self.s2, self.r2, p2_send.at[n], p2_recv.at[n], {"lat": across}
                )
                self.c3 = [
                    remote(
                        self.s3.at[d - 1], self.r3.at[d - 1],
                        p3_send.at[n3 + d - 1], p3_recv.at[n3 + d - 1],
                        {"lon": lax.rem(z + d, n_lon)},
                    )
                    for d in range(1, n_lon)
                ]
                self.c4 = remote(
                    self.g.at[y, core], self.g.at[y, core],
                    p4_send.at[n], p4_recv.at[n], {"lat": across},
                )
                self.c5 = [
                    remote(
                        self.g.at[h, core], self.g.at[h, core],
                        p5_send.at[2 * n + h], p5_recv.at[2 * n + h], {"lat": sibling},
                    )
                    for h in range(2)
                ]

            def first(self, fill):
                @pl.loop(0, 2)
                def _(k):
                    fill(2 * k + (1 - core), self.s1, k, BF16)

                self.c1.start()

                @pl.loop(0, 2)
                def _(k):
                    fill(2 * k + core, self.own, k, F32)

            def second(self):
                self.c1.wait()

                @pl.loop(0, n_lon)
                def _(q):
                    self.s2[q] = (self.own[1 - y, q] + self.r1[1 - y, q].astype(F32)).astype(BF16)

                self.c2.start()

                @pl.loop(0, n_lon)
                def _(q):
                    self.own[y, q] += self.r1[y, q].astype(F32)

            def third(self):
                self.c2.wait()
                for d in range(1, n_lon):
                    q = lax.rem(z + d, n_lon)
                    self.s3[d - 1] = (self.own[y, q] + self.r2[q].astype(F32)).astype(BF16)
                    self.c3[d - 1].start()

            def fourth(self):
                total = self.own[y, z] + self.r2[z].astype(F32)
                for d in range(1, n_lon):
                    self.c3[d - 1].wait()
                    total = total + self.r3[d - 1].astype(F32)
                self.g[y, core] = total * scale
                self.c4.start()

            def fifth(self):
                self.c4.wait()
                for c in self.c5:
                    c.start()

            def finish(self, put):
                for c in self.c5:
                    c.wait()
                for h in range(2):
                    for k in range(2):
                        put(2 * h + k, self.g[h, k])

        def spread(value, dst, k, dtype, lanes):
            for q in range(n_lon):
                dst[k, q, :, lanes] = value[q * share : (q + 1) * share].astype(dtype)

        def fill_own(l, dst, k, dtype):
            spread(dot(act[l], jg_ref[...], 0, 0), dst, k, dtype, slice(None))

        def fill_other(l, dst, k, dtype):
            spread(dot(act_in[l], jg_ref[...], 0, 0), dst, k, dtype, slice(None))

        def fill_conv(l, dst, k, dtype):
            grad = ps[1 : rows + 1, 1, l].reshape(cells, chans)
            for p in range(3):
                for q in range(3):
                    window = xs[p : p + rows, q, l].reshape(cells, chans)
                    tap = 3 * p + q
                    spread(
                        dot(window, grad, 0, 0), dst, k, dtype,
                        slice(tap * chans, (tap + 1) * chans),
                    )

        ra = Round(0, (own_a, s1_a, r1_a, s2_a, r2_a, s3_a, r3_a, g_a))
        rb = Round(1, (own_b, s1_b, r1_b, s2_b, r2_b, s3_b, r3_b, g_b))
        rc = Round(2, (own_c, s1_c, r1_c, s2_c, r2_c, s3_c, r3_c, g_c))

        ra.first(fill_own)
        rc.first(fill_conv)
        ra.second()
        for c in edges_g:
            c.wait()
        put_sides(1, ps)
        lat_start(1, ps)
        rc.second()
        act_copy.wait()
        rb.first(fill_other)
        ra.third()
        rb.second()
        lat_wait(1, ps)

        @pl.loop(0, levs)
        def _(l):
            total = None
            for p in range(3):
                for q in range(3):
                    window = ps[2 - p : 2 - p + rows, 2 - q, l].reshape(cells, chans)
                    term = dot(window, cw_ref[l, p, q], 1, 1)
                    total = term if total is None else total + term
            ig_ref[l] = total

        rc.third()
        own_cols = pl.ds(pl.multiple_of(e * wide, 128), wide)
        jf_ref[...] = jnp.zeros(jf_ref.shape, F32)

        @pl.loop(0, levs)
        def _(l):
            jf_ref[...] += dot(act[l], jw_ref[e * levs + l, :, own_cols], 1, 0)

        ra.fourth()
        rb.third()

        @pl.loop(0, levs)
        def _(l):
            jf_ref[...] += dot(act_in[l], jw_ref[(1 - e) * levs + l, :, own_cols], 1, 0)

        rc.fourth()
        ra.fifth()
        rb.fourth()
        rc.fifth()
        rb.fifth()

        def put_join(half):
            def put(i, value):
                gj_ref[half, i] = value

            return put

        def put_conv(i, value):
            gc_ref[i] = value

        ra.finish(put_join(e))
        rc.finish(put_conv)
        rb.finish(put_join(1 - e))

    def round_scratch(width):
        block = (n_lon, share, width)
        return [
            pltpu.VMEM((2,) + block, F32),
            pltpu.VMEM((2,) + block, BF16),
            pltpu.VMEM((2,) + block, BF16),
            pltpu.VMEM(block, BF16),
            pltpu.VMEM(block, BF16),
            pltpu.VMEM((n_lon - 1, share, width), BF16),
            pltpu.VMEM((n_lon - 1, share, width), BF16),
            pltpu.VMEM((2, 2, share, width), F32),
        ]

    dma = pltpu.SemaphoreType.DMA
    scratch = [
        pltpu.VMEM((cells, wide), BF16),
        pltpu.VMEM((4, levs, rows, chans), F32),
        pltpu.VMEM((4, levs, rows, chans), F32),
        pltpu.VMEM((rows + 2, 3, levs, cols, chans), BF16),
        pltpu.VMEM((rows + 2, 3, levs, cols, chans), BF16),
        pltpu.VMEM((levs, cells, chans), BF16),
        pltpu.VMEM((levs, cells, chans), BF16),
        pltpu.VMEM((levs, cells, chans), F32),
        *round_scratch(wide),
        *round_scratch(wide),
        *round_scratch(9 * chans),
        dma((2,)), dma((2,)), dma((4,)), dma((4,)), dma((4,)), dma((4,)),
        dma((3,)), dma((3,)), dma((3,)), dma((3,)),
        dma((3 * (n_lon - 1),)), dma((3 * (n_lon - 1),)),
        dma((3,)), dma((3,)), dma((6,)), dma((6,)),
    ]
    vmem = pl.BlockSpec(memory_space=pltpu.VMEM)
    return pl.pallas_call(
        kernel,
        out_shape=(
            jax.ShapeDtypeStruct((cells, wide), F32),
            jax.ShapeDtypeStruct((levs, cells, chans), F32),
            jax.ShapeDtypeStruct((2, levs, share, wide), F32),
            jax.ShapeDtypeStruct((levs, share, 9 * chans), F32),
        ),
        in_specs=[vmem] * 4,
        out_specs=(vmem,) * 4,
        scratch_shapes=scratch,
        compiler_params=pltpu.CompilerParams(
            collective_id=0, has_side_effects=True, vmem_limit_bytes=60 * 1024 * 1024
        ),
    )


def per_device(features, conv_weight, join_weight, joined_grad):
    rows, cols, levs, chans = features.shape
    lev_total = join_weight.shape[0]
    n_lon, n_lat = lax.axis_size("lon"), lax.axis_size("lat")
    share = chans // n_lon
    scale = 1.0 / math.sqrt(rows * n_lat * cols * n_lon)
    run = make_kernel(n_lon, n_lat, rows, cols, levs, chans, scale)
    jf, ig, gj, gc = run(
        jnp.transpose(features, (2, 0, 1, 3)),
        conv_weight,
        join_weight.reshape(lev_total, chans, lev_total * chans),
        joined_grad.reshape(rows * cols, levs * chans),
    )
    return (
        jf.reshape(features.shape),
        jnp.transpose(ig.reshape(levs, rows, cols, chans), (1, 2, 0, 3)),
        jnp.transpose(gc.reshape(levs, share, 3, 3, chans), (0, 2, 3, 1, 4)),
        gj.reshape(lev_total, share, levs, chans),
    )


def solution(mesh):
    in_specs = (
        P("lat", "lon", "lev", None),
        P("lev", None, None, None, None),
        P(),
        P("lat", "lon", "lev", None),
    )
    out_specs = (
        P("lat", "lon", "lev", None),
        P("lat", "lon", "lev", None),
        P("lev", None, None, "lon", None),
        P(None, "lon", "lev", None),
    )
    return jax.shard_map(
        per_device, mesh=mesh, in_specs=in_specs, out_specs=out_specs, check_vma=False
    )
```

```python
import math

import jax
import jax.numpy as jnp
from jax import lax
from jax.experimental import pallas as pl
from jax.experimental.pallas import tpu as pltpu
from jax.sharding import PartitionSpec as P

F32 = jnp.float32
BF16 = jnp.bfloat16
MESH = pl.DeviceIdType.MESH
ROOT = math.sqrt(2.0 / math.pi)


def dot(a, b, a_dim, b_dim):
    return lax.dot_general(a, b, (((a_dim,), (b_dim,)), ((), ())), preferred_element_type=F32)


def make_kernel(n_lon, n_lat, rows, cols, levs, chans, scale):
    share = chans // n_lon
    cells = rows * cols
    wide = levs * chans

    def kernel(
        x_ref, cw_ref, raw_ref, jg_ref,
        jf_ref, ig_ref, gj_ref, gc_ref,
        jg_in, edge_out, edge_in, xs, ps, act, act_in, ag,
        own_a, s1_a, r1_a, s2_a, r2_a, s3_a, r3_a, g_a,
        own_b, s1_b, r1_b, s2_b, r2_b, s3_b, r3_b, g_b,
        own_c, s1_c, r1_c, s2_c, r2_c, s3_c, r3_c, g_c,
        jw_ref, raw, loose, fields, jw_sem,
        lev_send, lev_recv, edge_send, edge_recv, lat_send, lat_recv,
        p1_send, p1_recv, p2_send, p2_recv, p3_send, p3_recv,
        p4_send, p4_recv, p5_send, p5_recv,
    ):
        z = lax.axis_index("lon")
        e = lax.axis_index("lev")
        t = lax.axis_index("lat")
        y = t // 2
        core = lax.rem(t, 2)
        right = lax.rem(z + 1, n_lon)
        left = lax.rem(z + n_lon - 1, n_lon)
        sibling = 2 * y + (1 - core)
        across = 2 * (1 - y) + core

        def jw_copy(l):
            return pltpu.make_async_copy(raw_ref.at[l], raw.at[l], jw_sem.at[l])

        @pl.loop(0, levs)
        def _(l):
            jw_copy(e * levs + l).start()

        @pl.loop(0, levs)
        def _(l):
            jw_copy((1 - e) * levs + l).start()

        def order_join(l):
            jw_copy(l).wait()
            for n, low in enumerate(range(0, chans, 128)):
                count = min(128, chans - low)
                loose[n, :, :count] = raw[l, :, low : low + count].astype(F32)
            for m in range(2 * levs):
                for n, low in enumerate(range(0, chans, 128)):
                    count = min(128, chans - low)
                    piece = loose.at[n][pl.ds(m, chans, stride=2 * levs), :]
                    first = m * chans + low
                    jw_ref[l, :, first : first + count] = piece[:, :count].astype(BF16)

        barrier = pltpu.get_barrier_semaphore()
        for d in range(1, n_lon):
            pl.semaphore_signal(
                barrier, inc=1, device_id={"lon": lax.rem(z + d, n_lon)}, device_id_type=MESH
            )
        for d in range(1, n_lat):
            pl.semaphore_signal(
                barrier, inc=1, device_id={"lat": lax.rem(t + d, n_lat)}, device_id_type=MESH
            )
        pl.semaphore_signal(barrier, inc=1, device_id={"lev": 1 - e}, device_id_type=MESH)
        pl.semaphore_wait(barrier, n_lon + n_lat - 1)

        def remote(src, dst, send, recv, where):
            return pltpu.make_async_remote_copy(
                src_ref=src, dst_ref=dst, send_sem=send, recv_sem=recv,
                device_id=where, device_id_type=MESH,
            )

        jg_copy = remote(jg_ref, jg_in, lev_send.at[0], lev_recv.at[0], {"lev": 1 - e})
        jg_copy.start()

        def edge_copies(n):
            return (
                remote(
                    edge_out.at[2 * n], edge_in.at[2 * n],
                    edge_send.at[2 * n], edge_recv.at[2 * n], {"lon": right},
                ),
                remote(
                    edge_out.at[2 * n + 1], edge_in.at[2 * n + 1],
                    edge_send.at[2 * n + 1], edge_recv.at[2 * n + 1], {"lon": left},
                ),
            )

        def put_middle(n, dst, l, value):
            edge_out[2 * n, l] = value[:, cols - 1, :]
            edge_out[2 * n + 1, l] = value[:, 0, :]
            dst[1 : rows + 1, 1, l] = value.astype(BF16)

        def put_sides(n, dst):
            @pl.loop(0, levs)
            def _(l):
                value = dst[1 : rows + 1, 1, l].astype(F32)
                before = edge_in[2 * n, l].reshape(rows, 1, chans)
                after = edge_in[2 * n + 1, l].reshape(rows, 1, chans)
                dst[1 : rows + 1, 0, l] = jnp.concatenate(
                    [before, value[:, : cols - 1]], axis=1
                ).astype(BF16)
                dst[1 : rows + 1, 2, l] = jnp.concatenate(
                    [value[:, 1:], after], axis=1
                ).astype(BF16)

        def lat_down(n, dst):
            return remote(
                dst.at[rows], dst.at[0], lat_send.at[2 * n], lat_recv.at[2 * n], {"lat": t + 1}
            )

        def lat_up(n, dst):
            return remote(
                dst.at[1], dst.at[rows + 1],
                lat_send.at[2 * n + 1], lat_recv.at[2 * n + 1], {"lat": t - 1},
            )

        def lat_start(n, dst):
            @pl.when(t < n_lat - 1)
            def _():
                lat_down(n, dst).start()

            @pl.when(t > 0)
            def _():
                lat_up(n, dst).start()

            @pl.when(t == 0)
            def _():
                dst[0] = jnp.zeros(dst.shape[1:], BF16)

            @pl.when(t == n_lat - 1)
            def _():
                dst[rows + 1] = jnp.zeros(dst.shape[1:], BF16)

        def lat_wait(n, dst):
            @pl.when(t < n_lat - 1)
            def _():
                lat_down(n, dst).wait_send()
                lat_up(n, dst).wait_recv()

            @pl.when(t > 0)
            def _():
                lat_up(n, dst).wait_send()
                lat_down(n, dst).wait_recv()

        @pl.loop(0, levs)
        def _(l):
            put_middle(0, xs, l, x_ref[l].astype(F32))

        edges = edge_copies(0)
        for c in edges:
            c.start()

        @pl.loop(0, levs)
        def _(l):
            order_join(e * levs + l)
            block = jw_ref[e * levs + l, :, pl.ds(pl.multiple_of(e * wide, 128), wide)]
            ag[l] = dot(jg_ref[...], block, 1, 1)

        for c in edges:
            c.wait()
        put_sides(0, xs)
        lat_start(0, xs)

        jg_copy.wait()

        @pl.loop(0, levs)
        def _(l):
            block = jw_ref[e * levs + l, :, pl.ds(pl.multiple_of((1 - e) * wide, 128), wide)]
            ag[l] += dot(jg_in[...], block, 1, 1)

        lat_wait(0, xs)

        @pl.loop(0, levs)
        def _(l):
            total = None
            for p in range(3):
                for q in range(3):
                    window = xs[p : p + rows, q, l].reshape(cells, chans)
                    term = dot(window, cw_ref[l, p, q], 1, 0)
                    total = term if total is None else total + term
            square = total * total
            bent = jnp.tanh(ROOT * (total + 0.044715 * total * square))
            half = 0.5 * (1.0 + bent)
            act[l] = (total * half).astype(BF16)
            slope = half + 0.5 * total * (1.0 - bent * bent) * (
                ROOT * (1.0 + 3.0 * 0.044715 * square)
            )
            grad = (ag[l] * slope).astype(BF16).astype(F32)
            put_middle(1, ps, l, grad.reshape(rows, cols, chans))

        act_copy = remote(act, act_in, lev_send.at[1], lev_recv.at[1], {"lev": 1 - e})
        act_copy.start()
        edges_g = edge_copies(1)
        for c in edges_g:
            c.start()

        class Round:
            def __init__(self, n, bufs):
                self.n = n
                self.own, self.s1, self.r1, self.s2, self.r2, self.s3, self.r3, self.g = bufs
                n3 = n * (n_lon - 1)
                self.c1 = remote(
                    self.s1, self.r1, p1_send.at[n], p1_recv.at[n], {"lat": sibling}
                )
                self.c2 = remote(
                    self.s2, self.r2, p2_send.at[n], p2_recv.at[n], {"lat": across}
                )
                self.c3 = [
                    remote(
                        self.s3.at[d - 1], self.r3.at[d - 1],
                        p3_send.at[n3 + d - 1], p3_recv.at[n3 + d - 1],
                        {"lon": lax.rem(z + d, n_lon)},
                    )
                    for d in range(1, n_lon)
                ]
                self.c4 = remote(
                    self.g.at[y, core], self.g.at[y, core],
                    p4_send.at[n], p4_recv.at[n], {"lat": across},
                )
                self.c5 = [
                    remote(
                        self.g.at[h, core], self.g.at[h, core],
                        p5_send.at[2 * n + h], p5_recv.at[2 * n + h], {"lat": sibling},
                    )
                    for h in range(2)
                ]

            def first(self, fill):
                @pl.loop(0, 2)
                def _(k):
                    fill(2 * k + (1 - core), self.s1, k, BF16)

                self.c1.start()

                @pl.loop(0, 2)
                def _(k):
                    fill(2 * k + core, self.own, k, F32)

            def second(self):
                self.c1.wait()

                @pl.loop(0, n_lon)
                def _(q):
                    self.s2[q] = (self.own[1 - y, q] + self.r1[1 - y, q].astype(F32)).astype(BF16)

                self.c2.start()

                @pl.loop(0, n_lon)
                def _(q):
                    self.own[y, q] += self.r1[y, q].astype(F32)

            def third(self):
                self.c2.wait()
                for d in range(1, n_lon):
                    q = lax.rem(z + d, n_lon)
                    self.s3[d - 1] = (self.own[y, q] + self.r2[q].astype(F32)).astype(BF16)
                    self.c3[d - 1].start()

            def fourth(self):
                total = self.own[y, z] + self.r2[z].astype(F32)
                for d in range(1, n_lon):
                    self.c3[d - 1].wait()
                    total = total + self.r3[d - 1].astype(F32)
                self.g[y, core] = total * scale
                self.c4.start()

            def fifth(self):
                self.c4.wait()
                for c in self.c5:
                    c.start()

            def finish(self, put):
                for c in self.c5:
                    c.wait()
                for h in range(2):
                    for k in range(2):
                        put(2 * h + k, self.g[h, k])

        def spread(value, dst, k, dtype, lanes):
            for q in range(n_lon):
                dst[k, q, :, lanes] = value[q * share : (q + 1) * share].astype(dtype)

        def fill_own(l, dst, k, dtype):
            spread(dot(act[l], jg_ref[...], 0, 0), dst, k, dtype, slice(None))

        def fill_other(l, dst, k, dtype):
            spread(dot(act_in[l], jg_ref[...], 0, 0), dst, k, dtype, slice(None))

        def fill_conv(l, dst, k, dtype):
            grad = ps[1 : rows + 1, 1, l].reshape(cells, chans)
            for p in range(3):
                for q in range(3):
                    window = xs[p : p + rows, q, l].reshape(cells, chans)
                    tap = 3 * p + q
                    spread(
                        dot(window, grad, 0, 0), dst, k, dtype,
                        slice(tap * chans, (tap + 1) * chans),
                    )

        ra = Round(0, (own_a, s1_a, r1_a, s2_a, r2_a, s3_a, r3_a, g_a))
        rb = Round(1, (own_b, s1_b, r1_b, s2_b, r2_b, s3_b, r3_b, g_b))
        rc = Round(2, (own_c, s1_c, r1_c, s2_c, r2_c, s3_c, r3_c, g_c))

        ra.first(fill_own)
        rc.first(fill_conv)
        ra.second()
        for c in edges_g:
            c.wait()
        put_sides(1, ps)
        lat_start(1, ps)
        rc.second()
        act_copy.wait()
        rb.first(fill_other)
        ra.third()
        rb.second()
        lat_wait(1, ps)

        @pl.loop(0, levs)
        def _(l):
            total = None
            for p in range(3):
                for q in range(3):
                    window = ps[2 - p : 2 - p + rows, 2 - q, l].reshape(cells, chans)
                    term = dot(window, cw_ref[l, p, q], 1, 1)
                    total = term if total is None else total + term
            ag[l] = total

        for l in range(levs):
            ig_ref[:, l, :] = ag[l]

        rc.third()
        own_cols = pl.ds(pl.multiple_of(e * wide, 128), wide)

        @pl.loop(0, levs)
        def _(l):
            order_join((1 - e) * levs + l)

        fields[...] = jnp.zeros(fields.shape, F32)

        @pl.loop(0, levs)
        def _(l):
            fields[...] += dot(act[l], jw_ref[e * levs + l, :, own_cols], 1, 0)

        ra.fourth()
        rb.third()

        @pl.loop(0, levs)
        def _(l):
            fields[...] += dot(act_in[l], jw_ref[(1 - e) * levs + l, :, own_cols], 1, 0)

        for m in range(levs):
            jf_ref[:, m, :] = fields[:, m * chans : (m + 1) * chans]

        rc.fourth()
        ra.fifth()
        rb.fourth()
        rc.fifth()
        rb.fifth()

        def put_join(half):
            def put(i, value):
                for m in range(levs):
                    gj_ref[half, i, :, m, :] = value[:, m * chans : (m + 1) * chans]

            return put

        def put_conv(i, value):
            for tap in range(9):
                gc_ref[i, tap // 3, tap % 3] = value[:, tap * chans : (tap + 1) * chans]

        ra.finish(put_join(e))
        rc.finish(put_conv)
        rb.finish(put_join(1 - e))

    def round_scratch(width):
        block = (n_lon, share, width)
        return [
            pltpu.VMEM((2,) + block, F32),
            pltpu.VMEM((2,) + block, BF16),
            pltpu.VMEM((2,) + block, BF16),
            pltpu.VMEM(block, BF16),
            pltpu.VMEM(block, BF16),
            pltpu.VMEM((n_lon - 1, share, width), BF16),
            pltpu.VMEM((n_lon - 1, share, width), BF16),
            pltpu.VMEM((2, 2, share, width), F32),
        ]

    dma = pltpu.SemaphoreType.DMA
    scratch = [
        pltpu.VMEM((cells, wide), BF16),
        pltpu.VMEM((4, levs, rows, chans), F32),
        pltpu.VMEM((4, levs, rows, chans), F32),
        pltpu.VMEM((rows + 2, 3, levs, cols, chans), BF16),
        pltpu.VMEM((rows + 2, 3, levs, cols, chans), BF16),
        pltpu.VMEM((levs, cells, chans), BF16),
        pltpu.VMEM((levs, cells, chans), BF16),
        pltpu.VMEM((levs, cells, chans), F32),
        *round_scratch(wide),
        *round_scratch(wide),
        *round_scratch(9 * chans),
        pltpu.VMEM((2 * levs, chans, 2 * wide), BF16),
        pltpu.VMEM((2 * levs, 2 * wide, chans), BF16),
        pltpu.VMEM((pl.cdiv(chans, 128), 2 * wide, 128), F32),
        pltpu.VMEM((cells, wide), F32),
        dma((2 * levs,)),
        dma((2,)), dma((2,)), dma((4,)), dma((4,)), dma((4,)), dma((4,)),
        dma((3,)), dma((3,)), dma((3,)), dma((3,)),
        dma((3 * (n_lon - 1),)), dma((3 * (n_lon - 1),)),
        dma((3,)), dma((3,)), dma((6,)), dma((6,)),
    ]
    vmem = pl.BlockSpec(memory_space=pltpu.VMEM)
    return pl.pallas_call(
        kernel,
        out_shape=(
            jax.ShapeDtypeStruct((cells, levs, chans), F32),
            jax.ShapeDtypeStruct((cells, levs, chans), F32),
            jax.ShapeDtypeStruct((2, levs, share, levs, chans), F32),
            jax.ShapeDtypeStruct((levs, 3, 3, share, chans), F32),
        ),
        in_specs=[vmem, vmem, pl.BlockSpec(memory_space=pl.ANY), vmem],
        out_specs=(vmem,) * 4,
        scratch_shapes=scratch,
        compiler_params=pltpu.CompilerParams(
            collective_id=0, has_side_effects=True, vmem_limit_bytes=60 * 1024 * 1024
        ),
    )


def per_device(features, conv_weight, join_weight, joined_grad):
    rows, cols, levs, chans = features.shape
    lev_total = join_weight.shape[0]
    n_lon, n_lat = lax.axis_size("lon"), lax.axis_size("lat")
    share = chans // n_lon
    scale = 1.0 / math.sqrt(rows * n_lat * cols * n_lon)
    run = make_kernel(n_lon, n_lat, rows, cols, levs, chans, scale)
    jf, ig, gj, gc = run(
        jnp.transpose(features, (2, 0, 1, 3)),
        conv_weight,
        join_weight.reshape(lev_total, chans * lev_total, chans),
        joined_grad.reshape(rows * cols, levs * chans),
    )
    return (
        jf.reshape(features.shape),
        ig.reshape(features.shape),
        gc,
        gj.reshape(lev_total, share, levs, chans),
    )


def solution(mesh):
    in_specs = (
        P("lat", "lon", "lev", None),
        P("lev", None, None, None, None),
        P(),
        P("lat", "lon", "lev", None),
    )
    out_specs = (
        P("lat", "lon", "lev", None),
        P("lat", "lon", "lev", None),
        P("lev", None, None, "lon", None),
        P(None, "lon", "lev", None),
    )
    return jax.shard_map(
        per_device, mesh=mesh, in_specs=in_specs, out_specs=out_specs, check_vma=False
    )
```

```python
import math

import jax
import jax.numpy as jnp
from jax import lax
from jax.experimental import pallas as pl
from jax.experimental.pallas import tpu as pltpu
from jax.sharding import PartitionSpec as P

F32 = jnp.float32
BF16 = jnp.bfloat16
MESH = pl.DeviceIdType.MESH
FIRST_TAPS = 4
ROOT = math.sqrt(2.0 / math.pi)


def dot(a, b, a_dim, b_dim):
    return lax.dot_general(a, b, (((a_dim,), (b_dim,)), ((), ())), preferred_element_type=F32)


def make_kernel(n_lon, n_lat, rows, cols, levs, chans, scale):
    share = chans // n_lon
    cells = rows * cols
    wide = levs * chans

    def kernel(
        x_ref, cw_ref, raw_ref, jg_ref,
        jf_ref, ig_ref, gj_ref, gc_ref,
        jg_in, edge_out, edge_in, xs, ps, act, act_in, ag,
        own_a, s1_a, r1_a, s2_a, r2_a, s3_a, r3_a, g_a,
        own_b, s1_b, r1_b, s2_b, r2_b, s3_b, r3_b, g_b,
        own_c, s1_c, r1_c, s2_c, r2_c, s3_c, r3_c, g_c,
        own_d, s1_d, r1_d, s2_d, r2_d, s3_d, r3_d, g_d,
        jw_ref, raw, loose, fields, slopes, jw_sem,
        lev_send, lev_recv, edge_send, edge_recv, lat_send, lat_recv,
        p1_send, p1_recv, p2_send, p2_recv, p3_send, p3_recv,
        p4_send, p4_recv, p5_send, p5_recv,
    ):
        z = lax.axis_index("lon")
        e = lax.axis_index("lev")
        t = lax.axis_index("lat")
        y = t // 2
        core = lax.rem(t, 2)
        right = lax.rem(z + 1, n_lon)
        left = lax.rem(z + n_lon - 1, n_lon)
        sibling = 2 * y + (1 - core)
        across = 2 * (1 - y) + core

        def jw_copy(l):
            return pltpu.make_async_copy(raw_ref.at[l], raw.at[l], jw_sem.at[l])

        @pl.loop(0, levs)
        def _(l):
            jw_copy(e * levs + l).start()

        @pl.loop(0, levs)
        def _(l):
            jw_copy((1 - e) * levs + l).start()

        def order_join(l):
            jw_copy(l).wait()
            for n, low in enumerate(range(0, chans, 128)):
                count = min(128, chans - low)
                loose[n, :, :count] = raw[l, :, low : low + count].astype(F32)
            for m in range(2 * levs):
                for n, low in enumerate(range(0, chans, 128)):
                    count = min(128, chans - low)
                    piece = loose.at[n][pl.ds(m, chans, stride=2 * levs), :]
                    first = m * chans + low
                    jw_ref[l, :, first : first + count] = piece[:, :count].astype(BF16)

        barrier = pltpu.get_barrier_semaphore()
        for d in range(1, n_lon):
            pl.semaphore_signal(
                barrier, inc=1, device_id={"lon": lax.rem(z + d, n_lon)}, device_id_type=MESH
            )
        for d in range(1, n_lat):
            pl.semaphore_signal(
                barrier, inc=1, device_id={"lat": lax.rem(t + d, n_lat)}, device_id_type=MESH
            )
        pl.semaphore_signal(barrier, inc=1, device_id={"lev": 1 - e}, device_id_type=MESH)
        pl.semaphore_wait(barrier, n_lon + n_lat - 1)

        def remote(src, dst, send, recv, where):
            return pltpu.make_async_remote_copy(
                src_ref=src, dst_ref=dst, send_sem=send, recv_sem=recv,
                device_id=where, device_id_type=MESH,
            )

        jg_copy = remote(jg_ref, jg_in, lev_send.at[0], lev_recv.at[0], {"lev": 1 - e})
        jg_copy.start()

        def edge_copies(n):
            return (
                remote(
                    edge_out.at[2 * n], edge_in.at[2 * n],
                    edge_send.at[2 * n], edge_recv.at[2 * n], {"lon": right},
                ),
                remote(
                    edge_out.at[2 * n + 1], edge_in.at[2 * n + 1],
                    edge_send.at[2 * n + 1], edge_recv.at[2 * n + 1], {"lon": left},
                ),
            )

        def put_middle(n, dst, l, value):
            edge_out[2 * n, l] = value[:, cols - 1, :]
            edge_out[2 * n + 1, l] = value[:, 0, :]
            dst[1 : rows + 1, 1, l] = value.astype(BF16)

        def put_sides(n, dst):
            @pl.loop(0, levs)
            def _(l):
                value = dst[1 : rows + 1, 1, l].astype(F32)
                before = edge_in[2 * n, l].reshape(rows, 1, chans)
                after = edge_in[2 * n + 1, l].reshape(rows, 1, chans)
                dst[1 : rows + 1, 0, l] = jnp.concatenate(
                    [before, value[:, : cols - 1]], axis=1
                ).astype(BF16)
                dst[1 : rows + 1, 2, l] = jnp.concatenate(
                    [value[:, 1:], after], axis=1
                ).astype(BF16)

        def lat_down(n, dst):
            return remote(
                dst.at[rows], dst.at[0], lat_send.at[2 * n], lat_recv.at[2 * n], {"lat": t + 1}
            )

        def lat_up(n, dst):
            return remote(
                dst.at[1], dst.at[rows + 1],
                lat_send.at[2 * n + 1], lat_recv.at[2 * n + 1], {"lat": t - 1},
            )

        def lat_start(n, dst):
            @pl.when(t < n_lat - 1)
            def _():
                lat_down(n, dst).start()

            @pl.when(t > 0)
            def _():
                lat_up(n, dst).start()

            @pl.when(t == 0)
            def _():
                dst[0] = jnp.zeros(dst.shape[1:], BF16)

            @pl.when(t == n_lat - 1)
            def _():
                dst[rows + 1] = jnp.zeros(dst.shape[1:], BF16)

        def lat_wait(n, dst):
            @pl.when(t < n_lat - 1)
            def _():
                lat_down(n, dst).wait_send()
                lat_up(n, dst).wait_recv()

            @pl.when(t > 0)
            def _():
                lat_up(n, dst).wait_send()
                lat_down(n, dst).wait_recv()

        @pl.loop(0, levs)
        def _(l):
            put_middle(0, xs, l, x_ref[l].astype(F32))

        edges = edge_copies(0)
        for c in edges:
            c.start()

        @pl.loop(0, levs)
        def _(l):
            order_join(e * levs + l)

        for c in edges:
            c.wait()
        put_sides(0, xs)
        lat_start(0, xs)

        @pl.loop(0, levs)
        def _(l):
            block = jw_ref[e * levs + l, :, pl.ds(pl.multiple_of(e * wide, 128), wide)]
            ag[l] = dot(jg_ref[...], block, 1, 1)

        lat_wait(0, xs)

        @pl.loop(0, levs)
        def _(l):
            total = None
            for p in range(3):
                for q in range(3):
                    window = xs[p : p + rows, q, l].reshape(cells, chans)
                    term = dot(window, cw_ref[l, p, q], 1, 0)
                    total = term if total is None else total + term
            square = total * total
            bent = jnp.tanh(ROOT * (total + 0.044715 * total * square))
            half = 0.5 * (1.0 + bent)
            act[l] = (total * half).astype(BF16)
            slopes[l] = half + 0.5 * total * (1.0 - bent * bent) * (
                ROOT * (1.0 + 3.0 * 0.044715 * square)
            )

        act_copy = remote(act, act_in, lev_send.at[1], lev_recv.at[1], {"lev": 1 - e})
        act_copy.start()

        class Round:
            def __init__(self, n, bufs):
                self.n = n
                self.own, self.s1, self.r1, self.s2, self.r2, self.s3, self.r3, self.g = bufs
                n3 = n * (n_lon - 1)
                self.c1 = remote(
                    self.s1, self.r1, p1_send.at[n], p1_recv.at[n], {"lat": sibling}
                )
                self.c2 = remote(
                    self.s2, self.r2, p2_send.at[n], p2_recv.at[n], {"lat": across}
                )
                self.c3 = [
                    remote(
                        self.s3.at[d - 1], self.r3.at[d - 1],
                        p3_send.at[n3 + d - 1], p3_recv.at[n3 + d - 1],
                        {"lon": lax.rem(z + d, n_lon)},
                    )
                    for d in range(1, n_lon)
                ]
                self.c4 = remote(
                    self.g.at[y, core], self.g.at[y, core],
                    p4_send.at[n], p4_recv.at[n], {"lat": across},
                )
                self.c5 = [
                    remote(
                        self.g.at[h, core], self.g.at[h, core],
                        p5_send.at[2 * n + h], p5_recv.at[2 * n + h], {"lat": sibling},
                    )
                    for h in range(2)
                ]

            def first(self, fill):
                @pl.loop(0, 2)
                def _(k):
                    fill(2 * k + (1 - core), self.s1, k, BF16)

                self.c1.start()

                @pl.loop(0, 2)
                def _(k):
                    fill(2 * k + core, self.own, k, F32)

            def second(self):
                self.c1.wait()

                @pl.loop(0, n_lon)
                def _(q):
                    self.s2[q] = (self.own[1 - y, q] + self.r1[1 - y, q].astype(F32)).astype(BF16)

                self.c2.start()

                @pl.loop(0, n_lon)
                def _(q):
                    self.own[y, q] += self.r1[y, q].astype(F32)

            def third(self):
                self.c2.wait()
                for d in range(1, n_lon):
                    q = lax.rem(z + d, n_lon)
                    self.s3[d - 1] = (self.own[y, q] + self.r2[q].astype(F32)).astype(BF16)
                    self.c3[d - 1].start()

            def fourth(self):
                total = self.own[y, z] + self.r2[z].astype(F32)
                for d in range(1, n_lon):
                    self.c3[d - 1].wait()
                    total = total + self.r3[d - 1].astype(F32)
                self.g[y, core] = total * scale
                self.c4.start()

            def fifth(self):
                self.c4.wait()
                for c in self.c5:
                    c.start()

            def finish(self, put):
                for c in self.c5:
                    c.wait()
                for h in range(2):
                    for k in range(2):
                        put(2 * h + k, self.g[h, k])

        def spread(value, dst, k, dtype, lanes):
            for q in range(n_lon):
                dst[k, q, :, lanes] = value[q * share : (q + 1) * share].astype(dtype)

        def fill_own(l, dst, k, dtype):
            spread(dot(act[l], jg_ref[...], 0, 0), dst, k, dtype, slice(None))

        def fill_other(l, dst, k, dtype):
            spread(dot(act_in[l], jg_ref[...], 0, 0), dst, k, dtype, slice(None))

        def fill_taps(taps):
            def fill(l, dst, k, dtype):
                grad = ps[1 : rows + 1, 1, l].reshape(cells, chans)
                for n, tap in enumerate(taps):
                    window = xs[tap // 3 : tap // 3 + rows, tap % 3, l].reshape(cells, chans)
                    spread(
                        dot(window, grad, 0, 0), dst, k, dtype,
                        slice(n * chans, (n + 1) * chans),
                    )

            return fill

        ra = Round(0, (own_a, s1_a, r1_a, s2_a, r2_a, s3_a, r3_a, g_a))
        rb = Round(1, (own_b, s1_b, r1_b, s2_b, r2_b, s3_b, r3_b, g_b))
        rc = Round(2, (own_c, s1_c, r1_c, s2_c, r2_c, s3_c, r3_c, g_c))
        rd = Round(3, (own_d, s1_d, r1_d, s2_d, r2_d, s3_d, r3_d, g_d))

        ra.first(fill_own)
        ra.second()
        jg_copy.wait()

        @pl.loop(0, levs)
        def _(l):
            block = jw_ref[e * levs + l, :, pl.ds(pl.multiple_of((1 - e) * wide, 128), wide)]
            total = ag[l] + dot(jg_in[...], block, 1, 1)
            grad = (total * slopes[l]).astype(BF16).astype(F32)
            put_middle(1, ps, l, grad.reshape(rows, cols, chans))

        edges_g = edge_copies(1)
        for c in edges_g:
            c.start()

        rc.first(fill_taps(range(FIRST_TAPS)))
        rc.second()
        for c in edges_g:
            c.wait()
        put_sides(1, ps)
        lat_start(1, ps)
        rd.first(fill_taps(range(FIRST_TAPS, 9)))
        ra.third()
        rd.second()
        act_copy.wait()
        rb.first(fill_other)
        rc.third()
        rb.second()

        @pl.loop(0, levs)
        def _(l):
            order_join((1 - e) * levs + l)

        ra.fourth()
        lat_wait(1, ps)

        @pl.loop(0, levs)
        def _(l):
            total = None
            for p in range(3):
                for q in range(3):
                    window = ps[2 - p : 2 - p + rows, 2 - q, l].reshape(cells, chans)
                    term = dot(window, cw_ref[l, p, q], 1, 1)
                    total = term if total is None else total + term
            ag[l] = total

        for l in range(levs):
            ig_ref[:, l, :] = ag[l]

        rd.third()
        ra.fifth()
        rc.fourth()
        own_cols = pl.ds(pl.multiple_of(e * wide, 128), wide)
        fields[...] = jnp.zeros(fields.shape, F32)

        @pl.loop(0, levs)
        def _(l):
            fields[...] += dot(act[l], jw_ref[e * levs + l, :, own_cols], 1, 0)

        rb.third()
        rc.fifth()

        @pl.loop(0, levs)
        def _(l):
            fields[...] += dot(act_in[l], jw_ref[(1 - e) * levs + l, :, own_cols], 1, 0)

        rd.fourth()

        for m in range(levs):
            jf_ref[:, m, :] = fields[:, m * chans : (m + 1) * chans]

        rb.fourth()
        rd.fifth()

        def put_join(half):
            def put(i, value):
                for m in range(levs):
                    gj_ref[half, i, :, m, :] = value[:, m * chans : (m + 1) * chans]

            return put

        def put_taps(taps):
            def put(i, value):
                for n, tap in enumerate(taps):
                    gc_ref[i, tap // 3, tap % 3] = value[:, n * chans : (n + 1) * chans]

            return put

        ra.finish(put_join(e))
        rc.finish(put_taps(range(FIRST_TAPS)))
        rb.fifth()
        rd.finish(put_taps(range(FIRST_TAPS, 9)))
        rb.finish(put_join(1 - e))

    def round_scratch(width):
        block = (n_lon, share, width)
        return [
            pltpu.VMEM((2,) + block, F32),
            pltpu.VMEM((2,) + block, BF16),
            pltpu.VMEM((2,) + block, BF16),
            pltpu.VMEM(block, BF16),
            pltpu.VMEM(block, BF16),
            pltpu.VMEM((n_lon - 1, share, width), BF16),
            pltpu.VMEM((n_lon - 1, share, width), BF16),
            pltpu.VMEM((2, 2, share, width), F32),
        ]

    dma = pltpu.SemaphoreType.DMA
    scratch = [
        pltpu.VMEM((cells, wide), BF16),
        pltpu.VMEM((4, levs, rows, chans), F32),
        pltpu.VMEM((4, levs, rows, chans), F32),
        pltpu.VMEM((rows + 2, 3, levs, cols, chans), BF16),
        pltpu.VMEM((rows + 2, 3, levs, cols, chans), BF16),
        pltpu.VMEM((levs, cells, chans), BF16),
        pltpu.VMEM((levs, cells, chans), BF16),
        pltpu.VMEM((levs, cells, chans), F32),
        *round_scratch(wide),
        *round_scratch(wide),
        *round_scratch(FIRST_TAPS * chans),
        *round_scratch((9 - FIRST_TAPS) * chans),
        pltpu.VMEM((2 * levs, chans, 2 * wide), BF16),
        pltpu.VMEM((2 * levs, 2 * wide, chans), BF16),
        pltpu.VMEM((pl.cdiv(chans, 128), 2 * wide, 128), F32),
        pltpu.VMEM((cells, wide), F32),
        pltpu.VMEM((levs, cells, chans), F32),
        dma((2 * levs,)),
        dma((2,)), dma((2,)), dma((4,)), dma((4,)), dma((4,)), dma((4,)),
        dma((4,)), dma((4,)), dma((4,)), dma((4,)),
        dma((4 * (n_lon - 1),)), dma((4 * (n_lon - 1),)),
        dma((4,)), dma((4,)), dma((8,)), dma((8,)),
    ]
    vmem = pl.BlockSpec(memory_space=pltpu.VMEM)
    return pl.pallas_call(
        kernel,
        out_shape=(
            jax.ShapeDtypeStruct((cells, levs, chans), F32),
            jax.ShapeDtypeStruct((cells, levs, chans), F32),
            jax.ShapeDtypeStruct((2, levs, share, levs, chans), F32),
            jax.ShapeDtypeStruct((levs, 3, 3, share, chans), F32),
        ),
        in_specs=[vmem, vmem, pl.BlockSpec(memory_space=pl.ANY), vmem],
        out_specs=(vmem,) * 4,
        scratch_shapes=scratch,
        compiler_params=pltpu.CompilerParams(
            collective_id=0, has_side_effects=True, vmem_limit_bytes=60 * 1024 * 1024
        ),
    )


def per_device(features, conv_weight, join_weight, joined_grad):
    rows, cols, levs, chans = features.shape
    lev_total = join_weight.shape[0]
    n_lon, n_lat = lax.axis_size("lon"), lax.axis_size("lat")
    share = chans // n_lon
    scale = 1.0 / math.sqrt(rows * n_lat * cols * n_lon)
    run = make_kernel(n_lon, n_lat, rows, cols, levs, chans, scale)
    jf, ig, gj, gc = run(
        jnp.transpose(features, (2, 0, 1, 3)),
        conv_weight,
        join_weight.reshape(lev_total, chans * lev_total, chans),
        joined_grad.reshape(rows * cols, levs * chans),
    )
    return (
        jf.reshape(features.shape),
        ig.reshape(features.shape),
        gc,
        gj.reshape(lev_total, share, levs, chans),
    )


def solution(mesh):
    in_specs = (
        P("lat", "lon", "lev", None),
        P("lev", None, None, None, None),
        P(),
        P("lat", "lon", "lev", None),
    )
    out_specs = (
        P("lat", "lon", "lev", None),
        P("lat", "lon", "lev", None),
        P("lev", None, None, "lon", None),
        P(None, "lon", "lev", None),
    )
    return jax.shard_map(
        per_device, mesh=mesh, in_specs=in_specs, out_specs=out_specs, check_vma=False
    )
```

```python
import math

import jax
import jax.numpy as jnp
from jax import lax
from jax.experimental import pallas as pl
from jax.experimental.pallas import tpu as pltpu
from jax.sharding import PartitionSpec as P

F32 = jnp.float32
BF16 = jnp.bfloat16
MESH = pl.DeviceIdType.MESH
FIRST_TAPS = 4
ROOT = math.sqrt(2.0 / math.pi)


def dot(a, b, a_dim, b_dim):
    return lax.dot_general(a, b, (((a_dim,), (b_dim,)), ((), ())), preferred_element_type=F32)


def make_kernel(n_lon, n_lat, rows, cols, levs, chans, scale):
    share = chans // n_lon
    cells = rows * cols
    wide = levs * chans

    def kernel(
        x_ref, cw_ref, raw_ref, grad_ref,
        jf_ref, ig_ref, gj_ref, gc_ref,
        jg_ref, by_cell, jg_in, edge_out, edge_in, xs, ps, act, act_in, ag,
        own_a, s1_a, r1_a, s2_a, r2_a, s3_a, r3_a, g_a,
        own_b, s1_b, r1_b, s2_b, r2_b, s3_b, r3_b, g_b,
        own_c, s1_c, r1_c, s2_c, r2_c, s3_c, r3_c, g_c,
        own_d, s1_d, r1_d, s2_d, r2_d, s3_d, r3_d, g_d,
        jw_ref, raw, loose, fields, slopes, jw_sem,
        lev_send, lev_recv, edge_send, edge_recv, lat_send, lat_recv,
        p1_send, p1_recv, p2_send, p2_recv, p3_send, p3_recv,
        p4_send, p4_recv, p5_send, p5_recv,
    ):
        z = lax.axis_index("lon")
        e = lax.axis_index("lev")
        t = lax.axis_index("lat")
        y = t // 2
        core = lax.rem(t, 2)
        right = lax.rem(z + 1, n_lon)
        left = lax.rem(z + n_lon - 1, n_lon)
        sibling = 2 * y + (1 - core)
        across = 2 * (1 - y) + core

        def jw_copy(l):
            return pltpu.make_async_copy(raw_ref.at[l], raw.at[l], jw_sem.at[l])

        @pl.loop(0, levs)
        def _(l):
            jw_copy(e * levs + l).start()

        @pl.loop(0, levs)
        def _(l):
            jw_copy((1 - e) * levs + l).start()

        def order_join(l):
            jw_copy(l).wait()
            for n, low in enumerate(range(0, chans, 128)):
                count = min(128, chans - low)
                loose[n, :, :count] = raw[l, :, low : low + count].astype(F32)
            for m in range(2 * levs):
                for n, low in enumerate(range(0, chans, 128)):
                    count = min(128, chans - low)
                    piece = loose.at[n][pl.ds(m, chans, stride=2 * levs), :]
                    first = m * chans + low
                    jw_ref[l, :, first : first + count] = piece[:, :count].astype(BF16)

        barrier = pltpu.get_barrier_semaphore()
        for d in range(1, n_lon):
            pl.semaphore_signal(
                barrier, inc=1, device_id={"lon": lax.rem(z + d, n_lon)}, device_id_type=MESH
            )
        for d in range(1, n_lat):
            pl.semaphore_signal(
                barrier, inc=1, device_id={"lat": lax.rem(t + d, n_lat)}, device_id_type=MESH
            )
        pl.semaphore_signal(barrier, inc=1, device_id={"lev": 1 - e}, device_id_type=MESH)
        pl.semaphore_wait(barrier, n_lon + n_lat - 1)

        def remote(src, dst, send, recv, where):
            return pltpu.make_async_remote_copy(
                src_ref=src, dst_ref=dst, send_sem=send, recv_sem=recv,
                device_id=where, device_id_type=MESH,
            )

        def edge_copies(n):
            return (
                remote(
                    edge_out.at[2 * n], edge_in.at[2 * n],
                    edge_send.at[2 * n], edge_recv.at[2 * n], {"lon": right},
                ),
                remote(
                    edge_out.at[2 * n + 1], edge_in.at[2 * n + 1],
                    edge_send.at[2 * n + 1], edge_recv.at[2 * n + 1], {"lon": left},
                ),
            )

        def put_middle(n, dst, l, value):
            edge_out[2 * n, l] = value[:, cols - 1, :]
            edge_out[2 * n + 1, l] = value[:, 0, :]
            dst[1 : rows + 1, 1, l] = value.astype(BF16)

        def put_sides(n, dst):
            @pl.loop(0, levs)
            def _(l):
                value = dst[1 : rows + 1, 1, l].astype(F32)
                before = edge_in[2 * n, l].reshape(rows, 1, chans)
                after = edge_in[2 * n + 1, l].reshape(rows, 1, chans)
                dst[1 : rows + 1, 0, l] = jnp.concatenate(
                    [before, value[:, : cols - 1]], axis=1
                ).astype(BF16)
                dst[1 : rows + 1, 2, l] = jnp.concatenate(
                    [value[:, 1:], after], axis=1
                ).astype(BF16)

        def lat_down(n, dst):
            return remote(
                dst.at[rows], dst.at[0], lat_send.at[2 * n], lat_recv.at[2 * n], {"lat": t + 1}
            )

        def lat_up(n, dst):
            return remote(
                dst.at[1], dst.at[rows + 1],
                lat_send.at[2 * n + 1], lat_recv.at[2 * n + 1], {"lat": t - 1},
            )

        def lat_start(n, dst):
            @pl.when(t < n_lat - 1)
            def _():
                lat_down(n, dst).start()

            @pl.when(t > 0)
            def _():
                lat_up(n, dst).start()

            @pl.when(t == 0)
            def _():
                dst[0] = jnp.zeros(dst.shape[1:], BF16)

            @pl.when(t == n_lat - 1)
            def _():
                dst[rows + 1] = jnp.zeros(dst.shape[1:], BF16)

        def lat_wait(n, dst):
            @pl.when(t < n_lat - 1)
            def _():
                lat_down(n, dst).wait_send()
                lat_up(n, dst).wait_recv()

            @pl.when(t > 0)
            def _():
                lat_up(n, dst).wait_send()
                lat_down(n, dst).wait_recv()

        by_cell[...] = x_ref[...].astype(F32)
        for l in range(levs):
            put_middle(0, xs, l, by_cell[:, l, :].reshape(rows, cols, chans))

        edges = edge_copies(0)
        for c in edges:
            c.start()

        by_cell[...] = grad_ref[...].astype(F32)
        for l in range(levs):
            jg_ref[:, l * chans : (l + 1) * chans] = by_cell[:, l, :].astype(BF16)

        jg_copy = remote(jg_ref, jg_in, lev_send.at[0], lev_recv.at[0], {"lev": 1 - e})
        jg_copy.start()

        @pl.loop(0, levs)
        def _(l):
            order_join(e * levs + l)

        for c in edges:
            c.wait()
        put_sides(0, xs)
        lat_start(0, xs)

        @pl.loop(0, levs)
        def _(l):
            block = jw_ref[e * levs + l, :, pl.ds(pl.multiple_of(e * wide, 128), wide)]
            ag[l] = dot(jg_ref[...], block, 1, 1)

        lat_wait(0, xs)

        @pl.loop(0, levs)
        def _(l):
            total = None
            for p in range(3):
                for q in range(3):
                    window = xs[p : p + rows, q, l].reshape(cells, chans)
                    term = dot(window, cw_ref[l, p, q], 1, 0)
                    total = term if total is None else total + term
            square = total * total
            bent = jnp.tanh(ROOT * (total + 0.044715 * total * square))
            half = 0.5 * (1.0 + bent)
            act[l] = (total * half).astype(BF16)
            slopes[l] = half + 0.5 * total * (1.0 - bent * bent) * (
                ROOT * (1.0 + 3.0 * 0.044715 * square)
            )

        act_copy = remote(act, act_in, lev_send.at[1], lev_recv.at[1], {"lev": 1 - e})
        act_copy.start()

        class Round:
            def __init__(self, n, bufs):
                self.n = n
                self.own, self.s1, self.r1, self.s2, self.r2, self.s3, self.r3, self.g = bufs
                n3 = n * (n_lon - 1)
                self.c1 = remote(
                    self.s1, self.r1, p1_send.at[n], p1_recv.at[n], {"lat": sibling}
                )
                self.c2 = remote(
                    self.s2, self.r2, p2_send.at[n], p2_recv.at[n], {"lat": across}
                )
                self.c3 = [
                    remote(
                        self.s3.at[d - 1], self.r3.at[d - 1],
                        p3_send.at[n3 + d - 1], p3_recv.at[n3 + d - 1],
                        {"lon": lax.rem(z + d, n_lon)},
                    )
                    for d in range(1, n_lon)
                ]
                self.c4 = remote(
                    self.g.at[y, core], self.g.at[y, core],
                    p4_send.at[n], p4_recv.at[n], {"lat": across},
                )
                self.c5 = [
                    remote(
                        self.g.at[h, core], self.g.at[h, core],
                        p5_send.at[2 * n + h], p5_recv.at[2 * n + h], {"lat": sibling},
                    )
                    for h in range(2)
                ]

            def first(self, fill):
                @pl.loop(0, 2)
                def _(k):
                    fill(2 * k + (1 - core), self.s1, k, BF16)

                self.c1.start()

                @pl.loop(0, 2)
                def _(k):
                    fill(2 * k + core, self.own, k, F32)

            def second(self):
                self.c1.wait()

                @pl.loop(0, n_lon)
                def _(q):
                    self.s2[q] = (self.own[1 - y, q] + self.r1[1 - y, q].astype(F32)).astype(BF16)

                self.c2.start()

                @pl.loop(0, n_lon)
                def _(q):
                    self.own[y, q] += self.r1[y, q].astype(F32)

            def third(self):
                self.c2.wait()
                for d in range(1, n_lon):
                    q = lax.rem(z + d, n_lon)
                    self.s3[d - 1] = (self.own[y, q] + self.r2[q].astype(F32)).astype(BF16)
                    self.c3[d - 1].start()

            def fourth(self):
                total = self.own[y, z] + self.r2[z].astype(F32)
                for d in range(1, n_lon):
                    self.c3[d - 1].wait()
                    total = total + self.r3[d - 1].astype(F32)
                self.g[y, core] = total * scale
                self.c4.start()

            def fifth(self):
                self.c4.wait()
                for c in self.c5:
                    c.start()

            def finish(self, put):
                for c in self.c5:
                    c.wait()
                for h in range(2):
                    for k in range(2):
                        put(2 * h + k, self.g[h, k])

        def spread(value, dst, k, dtype, lanes):
            for q in range(n_lon):
                dst[k, q, :, lanes] = value[q * share : (q + 1) * share].astype(dtype)

        def fill_own(l, dst, k, dtype):
            spread(dot(act[l], jg_ref[...], 0, 0), dst, k, dtype, slice(None))

        def fill_other(l, dst, k, dtype):
            spread(dot(act_in[l], jg_ref[...], 0, 0), dst, k, dtype, slice(None))

        def fill_taps(taps):
            def fill(l, dst, k, dtype):
                grad = ps[1 : rows + 1, 1, l].reshape(cells, chans)
                for n, tap in enumerate(taps):
                    window = xs[tap // 3 : tap // 3 + rows, tap % 3, l].reshape(cells, chans)
                    spread(
                        dot(window, grad, 0, 0), dst, k, dtype,
                        slice(n * chans, (n + 1) * chans),
                    )

            return fill

        ra = Round(0, (own_a, s1_a, r1_a, s2_a, r2_a, s3_a, r3_a, g_a))
        rb = Round(1, (own_b, s1_b, r1_b, s2_b, r2_b, s3_b, r3_b, g_b))
        rc = Round(2, (own_c, s1_c, r1_c, s2_c, r2_c, s3_c, r3_c, g_c))
        rd = Round(3, (own_d, s1_d, r1_d, s2_d, r2_d, s3_d, r3_d, g_d))

        ra.first(fill_own)
        ra.second()
        jg_copy.wait()

        @pl.loop(0, levs)
        def _(l):
            block = jw_ref[e * levs + l, :, pl.ds(pl.multiple_of((1 - e) * wide, 128), wide)]
            total = ag[l] + dot(jg_in[...], block, 1, 1)
            grad = (total * slopes[l]).astype(BF16).astype(F32)
            put_middle(1, ps, l, grad.reshape(rows, cols, chans))

        edges_g = edge_copies(1)
        for c in edges_g:
            c.start()

        rc.first(fill_taps(range(FIRST_TAPS)))
        rc.second()
        for c in edges_g:
            c.wait()
        put_sides(1, ps)
        lat_start(1, ps)
        rd.first(fill_taps(range(FIRST_TAPS, 9)))
        ra.third()
        rd.second()
        act_copy.wait()
        rb.first(fill_other)
        rc.third()
        rb.second()

        @pl.loop(0, levs)
        def _(l):
            order_join((1 - e) * levs + l)

        ra.fourth()
        lat_wait(1, ps)

        @pl.loop(0, levs)
        def _(l):
            total = None
            for p in range(3):
                for q in range(3):
                    window = ps[2 - p : 2 - p + rows, 2 - q, l].reshape(cells, chans)
                    term = dot(window, cw_ref[l, p, q], 1, 1)
                    total = term if total is None else total + term
            ag[l] = total

        for l in range(levs):
            ig_ref[:, l, :] = ag[l]

        rd.third()
        ra.fifth()
        rc.fourth()
        own_cols = pl.ds(pl.multiple_of(e * wide, 128), wide)
        fields[...] = jnp.zeros(fields.shape, F32)

        @pl.loop(0, levs)
        def _(l):
            fields[...] += dot(act[l], jw_ref[e * levs + l, :, own_cols], 1, 0)

        rb.third()
        rc.fifth()

        @pl.loop(0, levs)
        def _(l):
            fields[...] += dot(act_in[l], jw_ref[(1 - e) * levs + l, :, own_cols], 1, 0)

        rd.fourth()

        for m in range(levs):
            jf_ref[:, m, :] = fields[:, m * chans : (m + 1) * chans]

        rb.fourth()
        rd.fifth()

        def put_join(half):
            def put(i, value):
                for m in range(levs):
                    gj_ref[half, i, :, m, :] = value[:, m * chans : (m + 1) * chans]

            return put

        def put_taps(taps):
            def put(i, value):
                for n, tap in enumerate(taps):
                    gc_ref[i, tap // 3, tap % 3] = value[:, n * chans : (n + 1) * chans]

            return put

        ra.finish(put_join(e))
        rc.finish(put_taps(range(FIRST_TAPS)))
        rb.fifth()
        rd.finish(put_taps(range(FIRST_TAPS, 9)))
        rb.finish(put_join(1 - e))

    def round_scratch(width):
        block = (n_lon, share, width)
        return [
            pltpu.VMEM((2,) + block, F32),
            pltpu.VMEM((2,) + block, BF16),
            pltpu.VMEM((2,) + block, BF16),
            pltpu.VMEM(block, BF16),
            pltpu.VMEM(block, BF16),
            pltpu.VMEM((n_lon - 1, share, width), BF16),
            pltpu.VMEM((n_lon - 1, share, width), BF16),
            pltpu.VMEM((2, 2, share, width), F32),
        ]

    dma = pltpu.SemaphoreType.DMA
    scratch = [
        pltpu.VMEM((cells, wide), BF16),
        pltpu.VMEM((cells, levs, chans), F32),
        pltpu.VMEM((cells, wide), BF16),
        pltpu.VMEM((4, levs, rows, chans), F32),
        pltpu.VMEM((4, levs, rows, chans), F32),
        pltpu.VMEM((rows + 2, 3, levs, cols, chans), BF16),
        pltpu.VMEM((rows + 2, 3, levs, cols, chans), BF16),
        pltpu.VMEM((levs, cells, chans), BF16),
        pltpu.VMEM((levs, cells, chans), BF16),
        pltpu.VMEM((levs, cells, chans), F32),
        *round_scratch(wide),
        *round_scratch(wide),
        *round_scratch(FIRST_TAPS * chans),
        *round_scratch((9 - FIRST_TAPS) * chans),
        pltpu.VMEM((2 * levs, chans, 2 * wide), BF16),
        pltpu.VMEM((2 * levs, 2 * wide, chans), BF16),
        pltpu.VMEM((pl.cdiv(chans, 128), 2 * wide, 128), F32),
        pltpu.VMEM((cells, wide), F32),
        pltpu.VMEM((levs, cells, chans), F32),
        dma((2 * levs,)),
        dma((2,)), dma((2,)), dma((4,)), dma((4,)), dma((4,)), dma((4,)),
        dma((4,)), dma((4,)), dma((4,)), dma((4,)),
        dma((4 * (n_lon - 1),)), dma((4 * (n_lon - 1),)),
        dma((4,)), dma((4,)), dma((8,)), dma((8,)),
    ]
    vmem = pl.BlockSpec(memory_space=pltpu.VMEM)
    return pl.pallas_call(
        kernel,
        out_shape=(
            jax.ShapeDtypeStruct((cells, levs, chans), F32),
            jax.ShapeDtypeStruct((cells, levs, chans), F32),
            jax.ShapeDtypeStruct((2, levs, share, levs, chans), F32),
            jax.ShapeDtypeStruct((levs, 3, 3, share, chans), F32),
        ),
        in_specs=[vmem, vmem, pl.BlockSpec(memory_space=pl.ANY), vmem],
        out_specs=(vmem,) * 4,
        scratch_shapes=scratch,
        compiler_params=pltpu.CompilerParams(
            collective_id=0, has_side_effects=True, vmem_limit_bytes=60 * 1024 * 1024
        ),
    )


def per_device(features, conv_weight, join_weight, joined_grad):
    rows, cols, levs, chans = features.shape
    lev_total = join_weight.shape[0]
    n_lon, n_lat = lax.axis_size("lon"), lax.axis_size("lat")
    share = chans // n_lon
    scale = 1.0 / math.sqrt(rows * n_lat * cols * n_lon)
    run = make_kernel(n_lon, n_lat, rows, cols, levs, chans, scale)
    jf, ig, gj, gc = run(
        features.reshape(rows * cols, levs, chans),
        conv_weight,
        join_weight.reshape(lev_total, chans * lev_total, chans),
        joined_grad.reshape(rows * cols, levs, chans),
    )
    return (
        jf.reshape(features.shape),
        ig.reshape(features.shape),
        gc,
        gj.reshape(lev_total, share, levs, chans),
    )


def solution(mesh):
    in_specs = (
        P("lat", "lon", "lev", None),
        P("lev", None, None, None, None),
        P(),
        P("lat", "lon", "lev", None),
    )
    out_specs = (
        P("lat", "lon", "lev", None),
        P("lat", "lon", "lev", None),
        P("lev", None, None, "lon", None),
        P(None, "lon", "lev", None),
    )
    return jax.shard_map(
        per_device, mesh=mesh, in_specs=in_specs, out_specs=out_specs, check_vma=False
    )
```

```python
import math

import jax
import jax.numpy as jnp
from jax import lax
from jax.experimental import pallas as pl
from jax.experimental.pallas import tpu as pltpu
from jax.sharding import PartitionSpec as P

F32 = jnp.float32
BF16 = jnp.bfloat16
MESH = pl.DeviceIdType.MESH
FIRST_TAPS = 4
ROOT = math.sqrt(2.0 / math.pi)


def dot(a, b, a_dim, b_dim):
    return lax.dot_general(a, b, (((a_dim,), (b_dim,)), ((), ())), preferred_element_type=F32)


def make_kernel(n_lon, n_lat, rows, cols, levs, chans, scale):
    share = chans // n_lon
    cells = rows * cols
    wide = levs * chans

    def kernel(
        x_ref, cw_ref, raw_ref, grad_ref,
        jf_ref, ig_ref, gj_ref, gc_ref,
        jg_ref, by_cell, jg_in, edge_out, edge_in, xs, ps, act, act_in, ag,
        own_a, s1_a, r1_a, s2_a, r2_a, s3_a, r3_a, g_a,
        own_b, s1_b, r1_b, s2_b, r2_b, s3_b, r3_b, g_b,
        own_c, s1_c, r1_c, s2_c, r2_c, s3_c, r3_c, g_c,
        own_d, s1_d, r1_d, s2_d, r2_d, s3_d, r3_d, g_d,
        jw_ref, raw, loose, fields, slopes, jw_sem,
        lev_send, lev_recv, edge_send, edge_recv, lat_send, lat_recv,
        p1_send, p1_recv, p2_send, p2_recv, p3_send, p3_recv,
        p4_send, p4_recv, p5_send, p5_recv,
    ):
        z = lax.axis_index("lon")
        e = lax.axis_index("lev")
        t = lax.axis_index("lat")
        y = t // 2
        core = lax.rem(t, 2)
        right = lax.rem(z + 1, n_lon)
        left = lax.rem(z + n_lon - 1, n_lon)
        sibling = 2 * y + (1 - core)
        across = 2 * (1 - y) + core

        def jw_copy(l):
            return pltpu.make_async_copy(raw_ref.at[l], raw.at[l], jw_sem.at[l])

        @pl.loop(0, levs)
        def _(l):
            jw_copy(e * levs + l).start()

        @pl.loop(0, levs)
        def _(l):
            jw_copy((1 - e) * levs + l).start()

        def order_join(l):
            jw_copy(l).wait()
            for n, low in enumerate(range(0, chans, 128)):
                count = min(128, chans - low)
                loose[n, :, :count] = raw[l, :, low : low + count].astype(F32)
            for m in range(2 * levs):
                for n, low in enumerate(range(0, chans, 128)):
                    count = min(128, chans - low)
                    piece = loose.at[n][pl.ds(m, chans, stride=2 * levs), :]
                    first = m * chans + low
                    jw_ref[l, :, first : first + count] = piece[:, :count].astype(BF16)

        barrier = pltpu.get_barrier_semaphore()
        for d in range(1, n_lon):
            pl.semaphore_signal(
                barrier, inc=1, device_id={"lon": lax.rem(z + d, n_lon)}, device_id_type=MESH
            )
        for d in range(1, n_lat):
            pl.semaphore_signal(
                barrier, inc=1, device_id={"lat": lax.rem(t + d, n_lat)}, device_id_type=MESH
            )
        pl.semaphore_signal(barrier, inc=1, device_id={"lev": 1 - e}, device_id_type=MESH)
        pl.semaphore_wait(barrier, n_lon + n_lat - 1)

        def remote(src, dst, send, recv, where):
            return pltpu.make_async_remote_copy(
                src_ref=src, dst_ref=dst, send_sem=send, recv_sem=recv,
                device_id=where, device_id_type=MESH,
            )

        def edge_copies(n):
            return (
                remote(
                    edge_out.at[2 * n], edge_in.at[2 * n],
                    edge_send.at[2 * n], edge_recv.at[2 * n], {"lon": right},
                ),
                remote(
                    edge_out.at[2 * n + 1], edge_in.at[2 * n + 1],
                    edge_send.at[2 * n + 1], edge_recv.at[2 * n + 1], {"lon": left},
                ),
            )

        def put_middle(n, dst, l, value):
            edge_out[2 * n, l] = value[:, cols - 1, :]
            edge_out[2 * n + 1, l] = value[:, 0, :]
            dst[1 : rows + 1, 1, l] = value.astype(BF16)

        def put_sides(n, dst):
            @pl.loop(0, levs)
            def _(l):
                value = dst[1 : rows + 1, 1, l].astype(F32)
                before = edge_in[2 * n, l].reshape(rows, 1, chans)
                after = edge_in[2 * n + 1, l].reshape(rows, 1, chans)
                dst[1 : rows + 1, 0, l] = jnp.concatenate(
                    [before, value[:, : cols - 1]], axis=1
                ).astype(BF16)
                dst[1 : rows + 1, 2, l] = jnp.concatenate(
                    [value[:, 1:], after], axis=1
                ).astype(BF16)

        def lat_down(n, dst):
            return remote(
                dst.at[rows], dst.at[0], lat_send.at[2 * n], lat_recv.at[2 * n], {"lat": t + 1}
            )

        def lat_up(n, dst):
            return remote(
                dst.at[1], dst.at[rows + 1],
                lat_send.at[2 * n + 1], lat_recv.at[2 * n + 1], {"lat": t - 1},
            )

        def lat_start(n, dst):
            @pl.when(t < n_lat - 1)
            def _():
                lat_down(n, dst).start()

            @pl.when(t > 0)
            def _():
                lat_up(n, dst).start()

            @pl.when(t == 0)
            def _():
                dst[0] = jnp.zeros(dst.shape[1:], BF16)

            @pl.when(t == n_lat - 1)
            def _():
                dst[rows + 1] = jnp.zeros(dst.shape[1:], BF16)

        def lat_wait(n, dst):
            @pl.when(t < n_lat - 1)
            def _():
                lat_down(n, dst).wait_send()
                lat_up(n, dst).wait_recv()

            @pl.when(t > 0)
            def _():
                lat_up(n, dst).wait_send()
                lat_down(n, dst).wait_recv()

        by_cell[...] = x_ref[...].astype(F32)
        for l in range(levs):
            put_middle(0, xs, l, by_cell[:, l, :].reshape(rows, cols, chans))

        edges = edge_copies(0)
        for c in edges:
            c.start()

        by_cell[...] = grad_ref[...].astype(F32)
        for l in range(levs):
            jg_ref[:, l * chans : (l + 1) * chans] = by_cell[:, l, :].astype(BF16)

        jg_copy = remote(jg_ref, jg_in, lev_send.at[0], lev_recv.at[0], {"lev": 1 - e})
        jg_copy.start()

        @pl.loop(0, levs)
        def _(l):
            order_join(e * levs + l)

        for c in edges:
            c.wait()
        put_sides(0, xs)
        lat_start(0, xs)

        @pl.loop(0, levs)
        def _(l):
            block = jw_ref[e * levs + l, :, pl.ds(pl.multiple_of(e * wide, 128), wide)]
            ag[l] = dot(jg_ref[...], block, 1, 1)

        lat_wait(0, xs)

        @pl.loop(0, levs)
        def _(l):
            total = None
            for p in range(3):
                for q in range(3):
                    window = xs[p : p + rows, q, l].reshape(cells, chans)
                    term = dot(window, cw_ref[l, p, q], 1, 0)
                    total = term if total is None else total + term
            square = total * total
            bent = jnp.tanh(ROOT * (total + 0.044715 * total * square))
            half = 0.5 * (1.0 + bent)
            act[l] = (total * half).astype(BF16)
            slopes[l] = half + 0.5 * total * (1.0 - bent * bent) * (
                ROOT * (1.0 + 3.0 * 0.044715 * square)
            )

        act_copy = remote(act, act_in, lev_send.at[1], lev_recv.at[1], {"lev": 1 - e})
        act_copy.start()

        class Round:
            def __init__(self, n, bufs):
                self.n = n
                self.own, self.s1, self.r1, self.s2, self.r2, self.s3, self.r3, self.g = bufs
                n3 = n * (n_lon - 1)
                self.c1 = remote(
                    self.s1, self.r1, p1_send.at[n], p1_recv.at[n], {"lat": sibling}
                )
                self.c2 = remote(
                    self.s2, self.r2, p2_send.at[n], p2_recv.at[n], {"lat": across}
                )
                self.c3 = [
                    remote(
                        self.s3.at[d - 1], self.r3.at[d - 1],
                        p3_send.at[n3 + d - 1], p3_recv.at[n3 + d - 1],
                        {"lon": lax.rem(z + d, n_lon)},
                    )
                    for d in range(1, n_lon)
                ]
                self.c4 = remote(
                    self.g.at[y, core], self.g.at[y, core],
                    p4_send.at[n], p4_recv.at[n], {"lat": across},
                )
                self.c5 = [
                    remote(
                        self.g.at[h, core], self.g.at[h, core],
                        p5_send.at[2 * n + h], p5_recv.at[2 * n + h], {"lat": sibling},
                    )
                    for h in range(2)
                ]

            def first(self, fill):
                @pl.loop(0, 2)
                def _(k):
                    fill(2 * k + (1 - core), self.s1, k, BF16)

                self.c1.start()

                @pl.loop(0, 2)
                def _(k):
                    fill(2 * k + core, self.own, k, F32)

            def second(self):
                self.c1.wait()

                @pl.loop(0, n_lon)
                def _(q):
                    self.s2[q] = (self.own[1 - y, q] + self.r1[1 - y, q].astype(F32)).astype(BF16)

                self.c2.start()

                @pl.loop(0, n_lon)
                def _(q):
                    self.own[y, q] += self.r1[y, q].astype(F32)

            def third(self):
                self.c2.wait()
                for d in range(1, n_lon):
                    q = lax.rem(z + d, n_lon)
                    self.s3[d - 1] = (self.own[y, q] + self.r2[q].astype(F32)).astype(BF16)
                    self.c3[d - 1].start()

            def fourth(self):
                total = self.own[y, z] + self.r2[z].astype(F32)
                for d in range(1, n_lon):
                    self.c3[d - 1].wait()
                    total = total + self.r3[d - 1].astype(F32)
                self.g[y, core] = total * scale
                self.c4.start()

            def fifth(self):
                self.c4.wait()
                for c in self.c5:
                    c.start()

            def finish(self, put):
                for c in self.c5:
                    c.wait()
                for h in range(2):
                    for k in range(2):
                        put(2 * h + k, self.g[h, k])

        def spread(value, dst, k, dtype, lanes):
            for q in range(n_lon):
                dst[k, q, :, lanes] = value[q * share : (q + 1) * share].astype(dtype)

        def fill_own(l, dst, k, dtype):
            spread(dot(act[l], jg_ref[...], 0, 0), dst, k, dtype, slice(None))

        def fill_other(l, dst, k, dtype):
            spread(dot(act_in[l], jg_ref[...], 0, 0), dst, k, dtype, slice(None))

        def fill_taps(taps):
            def fill(l, dst, k, dtype):
                grad = ps[1 : rows + 1, 1, l].reshape(cells, chans)
                for n, tap in enumerate(taps):
                    window = xs[tap // 3 : tap // 3 + rows, tap % 3, l].reshape(cells, chans)
                    spread(
                        dot(window, grad, 0, 0), dst, k, dtype,
                        slice(n * chans, (n + 1) * chans),
                    )

            return fill

        ra = Round(0, (own_a, s1_a, r1_a, s2_a, r2_a, s3_a, r3_a, g_a))
        rb = Round(1, (own_b, s1_b, r1_b, s2_b, r2_b, s3_b, r3_b, g_b))
        rc = Round(2, (own_c, s1_c, r1_c, s2_c, r2_c, s3_c, r3_c, g_c))
        rd = Round(3, (own_d, s1_d, r1_d, s2_d, r2_d, s3_d, r3_d, g_d))

        ra.first(fill_own)
        ra.second()
        jg_copy.wait()

        @pl.loop(0, levs)
        def _(l):
            block = jw_ref[e * levs + l, :, pl.ds(pl.multiple_of((1 - e) * wide, 128), wide)]
            total = ag[l] + dot(jg_in[...], block, 1, 1)
            grad = (total * slopes[l]).astype(BF16).astype(F32)
            put_middle(1, ps, l, grad.reshape(rows, cols, chans))

        edges_g = edge_copies(1)
        for c in edges_g:
            c.start()

        rc.first(fill_taps(range(FIRST_TAPS)))
        rc.second()
        for c in edges_g:
            c.wait()
        put_sides(1, ps)
        lat_start(1, ps)
        rd.first(fill_taps(range(FIRST_TAPS, 9)))
        ra.third()
        rd.second()
        @pl.loop(0, levs)
        def _(l):
            order_join((1 - e) * levs + l)

        act_copy.wait()
        rb.first(fill_other)
        rc.third()
        rb.second()

        ra.fourth()
        lat_wait(1, ps)

        @pl.loop(0, levs)
        def _(l):
            total = None
            for p in range(3):
                for q in range(3):
                    window = ps[2 - p : 2 - p + rows, 2 - q, l].reshape(cells, chans)
                    term = dot(window, cw_ref[l, p, q], 1, 1)
                    total = term if total is None else total + term
            ag[l] = total

        for l in range(levs):
            ig_ref[:, l, :] = ag[l]

        rd.third()
        ra.fifth()
        rc.fourth()
        own_cols = pl.ds(pl.multiple_of(e * wide, 128), wide)
        fields[...] = jnp.zeros(fields.shape, F32)

        @pl.loop(0, levs)
        def _(l):
            fields[...] += dot(act[l], jw_ref[e * levs + l, :, own_cols], 1, 0)

        rb.third()
        rc.fifth()

        @pl.loop(0, levs)
        def _(l):
            fields[...] += dot(act_in[l], jw_ref[(1 - e) * levs + l, :, own_cols], 1, 0)

        rd.fourth()

        for m in range(levs):
            jf_ref[:, m, :] = fields[:, m * chans : (m + 1) * chans]

        rb.fourth()
        rd.fifth()

        def put_join(half):
            def put(i, value):
                for m in range(levs):
                    gj_ref[half, i, :, m, :] = value[:, m * chans : (m + 1) * chans]

            return put

        def put_taps(taps):
            def put(i, value):
                for n, tap in enumerate(taps):
                    gc_ref[i, tap // 3, tap % 3] = value[:, n * chans : (n + 1) * chans]

            return put

        ra.finish(put_join(e))
        rc.finish(put_taps(range(FIRST_TAPS)))
        rb.fifth()
        rd.finish(put_taps(range(FIRST_TAPS, 9)))
        rb.finish(put_join(1 - e))

    def round_scratch(width):
        block = (n_lon, share, width)
        return [
            pltpu.VMEM((2,) + block, F32),
            pltpu.VMEM((2,) + block, BF16),
            pltpu.VMEM((2,) + block, BF16),
            pltpu.VMEM(block, BF16),
            pltpu.VMEM(block, BF16),
            pltpu.VMEM((n_lon - 1, share, width), BF16),
            pltpu.VMEM((n_lon - 1, share, width), BF16),
            pltpu.VMEM((2, 2, share, width), F32),
        ]

    dma = pltpu.SemaphoreType.DMA
    scratch = [
        pltpu.VMEM((cells, wide), BF16),
        pltpu.VMEM((cells, levs, chans), F32),
        pltpu.VMEM((cells, wide), BF16),
        pltpu.VMEM((4, levs, rows, chans), F32),
        pltpu.VMEM((4, levs, rows, chans), F32),
        pltpu.VMEM((rows + 2, 3, levs, cols, chans), BF16),
        pltpu.VMEM((rows + 2, 3, levs, cols, chans), BF16),
        pltpu.VMEM((levs, cells, chans), BF16),
        pltpu.VMEM((levs, cells, chans), BF16),
        pltpu.VMEM((levs, cells, chans), F32),
        *round_scratch(wide),
        *round_scratch(wide),
        *round_scratch(FIRST_TAPS * chans),
        *round_scratch((9 - FIRST_TAPS) * chans),
        pltpu.VMEM((2 * levs, chans, 2 * wide), BF16),
        pltpu.VMEM((2 * levs, 2 * wide, chans), BF16),
        pltpu.VMEM((pl.cdiv(chans, 128), 2 * wide, 128), F32),
        pltpu.VMEM((cells, wide), F32),
        pltpu.VMEM((levs, cells, chans), F32),
        dma((2 * levs,)),
        dma((2,)), dma((2,)), dma((4,)), dma((4,)), dma((4,)), dma((4,)),
        dma((4,)), dma((4,)), dma((4,)), dma((4,)),
        dma((4 * (n_lon - 1),)), dma((4 * (n_lon - 1),)),
        dma((4,)), dma((4,)), dma((8,)), dma((8,)),
    ]
    vmem = pl.BlockSpec(memory_space=pltpu.VMEM)
    return pl.pallas_call(
        kernel,
        out_shape=(
            jax.ShapeDtypeStruct((cells, levs, chans), F32),
            jax.ShapeDtypeStruct((cells, levs, chans), F32),
            jax.ShapeDtypeStruct((2, levs, share, levs, chans), F32),
            jax.ShapeDtypeStruct((levs, 3, 3, share, chans), F32),
        ),
        in_specs=[vmem, vmem, pl.BlockSpec(memory_space=pl.ANY), vmem],
        out_specs=(vmem,) * 4,
        scratch_shapes=scratch,
        compiler_params=pltpu.CompilerParams(
            collective_id=0, has_side_effects=True, vmem_limit_bytes=60 * 1024 * 1024
        ),
    )


def per_device(features, conv_weight, join_weight, joined_grad):
    rows, cols, levs, chans = features.shape
    lev_total = join_weight.shape[0]
    n_lon, n_lat = lax.axis_size("lon"), lax.axis_size("lat")
    share = chans // n_lon
    scale = 1.0 / math.sqrt(rows * n_lat * cols * n_lon)
    run = make_kernel(n_lon, n_lat, rows, cols, levs, chans, scale)
    jf, ig, gj, gc = run(
        features.reshape(rows * cols, levs, chans),
        conv_weight,
        join_weight.reshape(lev_total, chans * lev_total, chans),
        joined_grad.reshape(rows * cols, levs, chans),
    )
    return (
        jf.reshape(features.shape),
        ig.reshape(features.shape),
        gc,
        gj.reshape(lev_total, share, levs, chans),
    )


def solution(mesh):
    in_specs = (
        P("lat", "lon", "lev", None),
        P("lev", None, None, None, None),
        P(),
        P("lat", "lon", "lev", None),
    )
    out_specs = (
        P("lat", "lon", "lev", None),
        P("lat", "lon", "lev", None),
        P("lev", None, None, "lon", None),
        P(None, "lon", "lev", None),
    )
    return jax.shard_map(
        per_device, mesh=mesh, in_specs=in_specs, out_specs=out_specs, check_vma=False
    )
```
